512 devices in a mesh: ia: 4 (over z_hi), ja: 16 (over z_lo, y), ka: 8 (over x, core).
Axes of the slice: x: 4, y: 8, z: 8 (z_hi: 4, z_lo: 2; z = z_hi * 2 + z_lo), core: 2. Of those that a mesh axis runs over, the one named last changes fastest.
Arguments:
- tensor: float32 [32, 2048, 4096], P('ka', 'ia', 'ja'), may hold values from -6 to 6
- factor_b: float32 [4096, 64], P(('ja', 'ka')), may hold values from -0.09375 to 0.09375
- factor_c: float32 [32, 64], P('ka'), may hold values from -1 to 1
Outputs:
- update: float32 [2048, 64], P(('ia', 'ja', 'ka'))
The draws below stay inside these ranges and needn't reach their ends.
All inputs are finite; a program needn't handle non-finite values.
Results may differ from the reference program's by a relative error of at most 0.00011.
Values sent between devices are 32-bit elements; how exact they have to be, the bound alone decides.
No kernel may reach another device: no remote copies, remote signals or barrier semaphores. Data moves between devices by JAX's collectives and lax.ppermute only.
A program may use at most 64 MiB of HBM per device.

```python
import jax
import jax.numpy as jnp
from jax import lax

R = 64
I = 2048
J = 4096
K = 32


def level_of(stream_key, shape, split, low, top_value):
    loudness = 1.0
    for axis_at, shards_of in split:
        heights = jax.random.uniform(jax.random.fold_in(jax.random.fold_in(stream_key, 6), axis_at), (shards_of,), jnp.float32, low / len(split), top_value / len(split))
        loudness = loudness * jnp.repeat(jnp.exp(heights), shape[axis_at] // shards_of).reshape((-1,) + (1,) * (len(shape) - 1 - axis_at))
    return loudness


def bell_draw(rng, dims, deviation, reach, split=(), dtype=jnp.bfloat16):
    entries = deviation * jax.random.normal(rng, dims, jnp.float32)
    if split:
        entries = entries * level_of(rng, dims, split, -0.22, 0.18)
    return jnp.clip(entries, -reach, reach).astype(dtype)


def setup_inputs(seed: int = 0) -> dict:
    streams_of = jax.random.split(jax.random.key(seed), 4)
    return {
        "tensor": bell_draw(streams_of[0], (K, I, J), 1.0, 6.0, ((0, 8), (1, 4), (2, 16)), jnp.float32),
        "factor_b": bell_draw(streams_of[1], (J, R), J ** -0.5, 0.09375, ((0, 128),), jnp.float32),
        "factor_c": bell_draw(streams_of[2], (K, R), K ** -0.5, 1.0, ((0, 8),), jnp.float32),
    }


def depth_partial(tensor_slice, factor_b):
    return jnp.dot(tensor_slice.astype(jnp.float32), factor_b.astype(jnp.float32), precision=lax.Precision.HIGHEST, preferred_element_type=jnp.float32)

def reference(tensor, factor_b, factor_c):
    partial_value = lax.map(lambda piece: depth_partial(piece, factor_b), tensor)
    mttkrp = jnp.einsum('kir,kr->ir', partial_value, factor_c, precision=lax.Precision.HIGHEST)
    gram_b = jnp.dot(factor_b.T.astype(jnp.float32), factor_b.astype(jnp.float32), precision=lax.Precision.HIGHEST, preferred_element_type=jnp.float32)
    gram_c = jnp.dot(factor_c.T.astype(jnp.float32), factor_c.astype(jnp.float32), precision=lax.Precision.HIGHEST, preferred_element_type=jnp.float32)
    gram = gram_b * gram_c
    lower = jnp.linalg.cholesky(gram)
    solved = jax.scipy.linalg.cho_solve((lower, True), mttkrp.T)
    return solved.T
```

```python
import jax
import jax.numpy as jnp
from jax import lax
from jax.sharding import PartitionSpec as P

HI = lax.Precision.HIGHEST


def per_device(tensor, factor_b, factor_c):
    n_ja, n_ka = lax.axis_size("ja"), lax.axis_size("ka")
    rows_b, rank = factor_b.shape
    depth = factor_c.shape[0]
    mine = jnp.concatenate([factor_b, factor_c], axis=0)
    block = lax.all_to_all(
        jnp.broadcast_to(mine[None], (n_ka,) + mine.shape), "ka", 0, 0, tiled=True
    )
    b_block = block[:, :rows_b].reshape(n_ka * rows_b, rank)
    c_all = block[:, rows_b:].reshape(n_ka * depth, rank)
    partial_value = jnp.einsum("kij,jr->kir", tensor, b_block, precision=HI)
    local_sums = jnp.einsum("kir,kr->ir", partial_value, factor_c, precision=HI)
    gram = jnp.dot(b_block.T, b_block, precision=HI) * jnp.dot(c_all.T, c_all, precision=HI)
    peers = n_ja * n_ka
    sums_part = local_sums.reshape(peers, -1)
    piece = rank // n_ka
    gram_part = lax.dynamic_slice_in_dim(gram, lax.axis_index("ka") * piece, piece, 0)
    gram_part = jnp.broadcast_to(gram_part.reshape(1, -1), (peers, piece * rank))
    got = lax.all_to_all(
        jnp.concatenate([sums_part, gram_part], axis=1), ("ja", "ka"), 0, 0, tiled=True
    )
    owned = jnp.sum(got[:, : sums_part.shape[1]], axis=0).reshape(-1, rank)
    gram = jnp.sum(got[:, sums_part.shape[1] :].reshape(n_ja, n_ka, -1), axis=0).reshape(rank, rank)
    lower = jnp.linalg.cholesky(gram)
    solved = jax.scipy.linalg.cho_solve((lower, True), owned.T)
    return solved.T


def solution(mesh):
    in_specs = (P("ka", "ia", "ja"), P(("ja", "ka"), None), P("ka", None))
    out_specs = P(("ia", "ja", "ka"), None)
    return jax.shard_map(
        per_device, mesh=mesh, in_specs=in_specs, out_specs=out_specs, check_vma=False
    )
```

```python
import functools

import jax
import jax.numpy as jnp
from jax import lax
from jax.experimental import pallas as pl
from jax.experimental.pallas import tpu as pltpu
from jax.sharding import PartitionSpec as P

HI = lax.Precision.HIGHEST
F32, B16 = jnp.float32, jnp.bfloat16
VMEM = pltpu.VMEM


def spread(n_ka, b_ref, c_ref, out_ref):
    rows, rank = b_ref.shape
    b = jnp.concatenate([b_ref[: rows // 2], b_ref[rows // 2 :]], axis=1)
    c = jnp.concatenate([c_ref[...], jnp.zeros((8 - c_ref.shape[0], rank), F32)], axis=0)
    c = jnp.concatenate([c, c], axis=1)
    for peer in range(n_ka):
        out_ref[peer, : rows // 2] = b
        out_ref[peer, rows // 2 :] = c


def split(x):
    high = x.astype(B16)
    return high, (x - high.astype(F32)).astype(B16)


def transposed_dot(x, y):
    return lax.dot_general(x, y, (((0,), (0,)), ((), ())), precision=HI, preferred_element_type=F32)


def pack(n_ja, n_ka, t_ref, block_ref, c_ref, out_ref, gram_ref, sums_ref):
    ka = lax.axis_index("ka")
    peers = n_ja * n_ka
    depth, rows, cols = t_ref.shape
    rank = c_ref.shape[1]
    half = rank // 2
    b = jnp.concatenate([block_ref[:, :-8, :rank], block_ref[:, :-8, rank:]], axis=1).reshape(-1, rank)
    c_wide = block_ref[:, -8:].reshape(-1, 2 * rank)
    c_all = c_wide[:, :rank]
    wide = jnp.concatenate([b, b], axis=1)
    gram_ref[...] = transposed_dot(b, wide) * transposed_dot(c_all, c_wide)
    weights = []
    for k in range(depth):
        high, low = split(b * c_ref[k : k + 1, :])
        weights.append((high, jnp.concatenate([high, low], axis=1)))
    per = rows // peers
    step = rows // 4
    for at in range(0, rows, step):
        first = jnp.zeros((step, 2 * rank), F32)
        second = jnp.zeros((step, rank), F32)
        for k in range(depth):
            high, low = split(t_ref[k, at : at + step, :])
            first += jnp.dot(high, weights[k][1], preferred_element_type=F32)
            second += jnp.dot(low, weights[k][0], preferred_element_type=F32)
        sums_ref[at : at + step, :rank] = first[:, :rank] + (first[:, rank:] + second)
    lane = lax.broadcasted_iota(jnp.int32, (peers, 2 * rank), 1)
    for q in range(per):
        row = gram_ref[pl.ds(ka + 8 * q, 1), :]
        out_ref[pl.ds(q, peers, stride=5), :] = jnp.where(
            lane < rank, sums_ref[pl.ds(q, peers, stride=per), :], row
        )
    last = jnp.zeros((1, 2 * rank), F32)
    one = lax.broadcasted_iota(jnp.int32, (1, 2 * rank), 1)
    for q in range(4):
        row = gram_ref[pl.ds(half + ka + 8 * q, 1), :]
        row = pltpu.roll(row, (half * q - half) % (2 * rank), 1)
        last = jnp.where(one // half == q, row, last)
    out_ref[pl.ds(4, peers, stride=5), :] = jnp.broadcast_to(last, (peers, 2 * rank))


def inverse(x):
    r = pl.reciprocal(x, approx=True)
    r = r * (2.0 - x * r)
    return r * (2.0 - x * r)


def solve(n_ja, n_ka, got_ref, out_ref, sum_ref):
    rank = 64
    half = rank // 2
    wide = 2 * rank
    per = n_ka * 5
    parts = [got_ref[pl.ds(a * per, per), :] for a in range(n_ja)]
    while len(parts) > 1:
        parts = [x + y for x, y in zip(parts[::2], parts[1::2])]
    sum_ref[...] = parts[0]
    x = [sum_ref[pl.ds(q, n_ka, stride=5), :] for q in range(5)]
    lane = lax.broadcasted_iota(jnp.int32, (8, wide), 1)
    sub = lax.broadcasted_iota(jnp.int32, (8, wide), 0)
    upper = jnp.concatenate(x[:4], axis=0)
    flipped = jnp.transpose(upper)[rank + half :, :]
    groups = []
    for g in range(8):
        eye = jnp.where(lane == 8 * g + sub, 1.0, 0.0)
        if g < 4:
            right = x[g]
        else:
            corner = pltpu.roll(x[4], (96 - half * (g - 4)) % wide, 1)
            lower = flipped[8 * (g - 4) : 8 * (g - 3), :]
            lower = jnp.concatenate([lower] * 4, axis=1)
            right = jnp.where(lane < rank + half, lower, corner)
        groups.append(jnp.where(lane < rank, eye, right))
    sums = [jnp.sum(x[q], axis=0, keepdims=True) for q in range(4)]
    m = jnp.concatenate(sums + [jnp.zeros((4, wide), F32)], axis=0)
    m = pltpu.roll(m, rank, 1)
    groups.append(jnp.where(lane < rank, 0.0, m))

    def column(a, c):
        return jnp.broadcast_to(a[:, c : c + 1], (8, wide))

    def row(a, r):
        return jnp.broadcast_to(a[r : r + 1, :], (8, wide))

    for r in range(8):
        at = rank + 8 * r
        own = groups[r]
        cols = [column(own, at + s) for s in range(8)]
        pivots = {(u, v): row(cols[v], u) for u in range(8) for v in range(u + 1)}
        rows = [row(own, s) for s in range(8)]
        left = {g: [column(groups[g], at + s) for s in range(8)] for g in range(r + 1, 9)}
        for t in range(8):
            inv = inverse(pivots[t, t])
            scaled = rows[t] * inv
            ratio = {u: pivots[u, t] * inv for u in range(t + 1, 8)}
            for u in range(t + 1, 8):
                for v in range(t + 1, u + 1):
                    pivots[u, v] = pivots[u, v] - ratio[u] * pivots[v, t]
            for u in range(t + 1, 8):
                rows[u] = rows[u] - ratio[u] * rows[t]
            for g in range(r + 1, 9):
                groups[g] = groups[g] - left[g][t] * scaled
                for u in range(t + 1, 8):
                    left[g][u] = left[g][u] - ratio[u] * left[g][t]
    out_ref[...] = -groups[8][: out_ref.shape[0], :rank]


def per_device(tensor, factor_b, factor_c):
    n_ja, n_ka = lax.axis_size("ja"), lax.axis_size("ka")
    peers = n_ja * n_ka
    rows_b, rank = factor_b.shape
    mine = pl.pallas_call(
        functools.partial(spread, n_ka),
        out_shape=jax.ShapeDtypeStruct((n_ka, rows_b // 2 + 8, 2 * rank), F32),
        name="spread",
    )(factor_b, factor_c)
    block = lax.all_to_all(mine, "ka", 0, 0, tiled=True)
    packed = pl.pallas_call(
        functools.partial(pack, n_ja, n_ka),
        out_shape=jax.ShapeDtypeStruct((peers * 5, 2 * rank), F32),
        scratch_shapes=[
            pltpu.VMEM((rank, 2 * rank), F32),
            pltpu.VMEM((tensor.shape[1], 2 * rank), F32),
        ],
        compiler_params=pltpu.CompilerParams(vmem_limit_bytes=32 * 2**20),
        name="pack",
    )(tensor, block, factor_c)
    got = lax.all_to_all(packed.reshape(peers, 1, 10 * rank), ("ja", "ka"), 0, 0, tiled=True)
    return pl.pallas_call(
        functools.partial(solve, n_ja, n_ka),
        out_shape=jax.ShapeDtypeStruct((tensor.shape[1] // peers, rank), F32),
        scratch_shapes=[pltpu.VMEM((n_ka * 5, 2 * rank), F32)],
        compiler_params=pltpu.CompilerParams(vmem_limit_bytes=32 * 2**20),
        name="solve",
    )(got.reshape(peers * 5, 2 * rank))


def solution(mesh):
    in_specs = (P("ka", "ia", "ja"), P(("ja", "ka"), None), P("ka", None))
    out_specs = P(("ia", "ja", "ka"), None)
    return jax.shard_map(
        per_device, mesh=mesh, in_specs=in_specs, out_specs=out_specs, check_vma=False
    )
```

```python
import functools

import jax
import jax.numpy as jnp
from jax import lax
from jax.experimental import pallas as pl
from jax.experimental.pallas import tpu as pltpu
from jax.sharding import Mesh
from jax.sharding import PartitionSpec as P

HI = lax.Precision.HIGHEST
F32, B16 = jnp.float32, jnp.bfloat16
BIG = pltpu.CompilerParams(vmem_limit_bytes=32 * 2**20)


def spread(n_ka, b_ref, c_ref, out_ref):
    rows, rank = b_ref.shape
    b = jnp.concatenate([b_ref[: rows // 2], b_ref[rows // 2 :]], axis=1)
    c = jnp.concatenate([c_ref[...], jnp.zeros((8 - c_ref.shape[0], rank), F32)], axis=0)
    c = jnp.concatenate([c, c], axis=1)
    for peer in range(n_ka):
        out_ref[peer, : rows // 2] = b
        out_ref[peer, rows // 2 :] = c


def split(x):
    high = x.astype(B16)
    return high, (x - high.astype(F32)).astype(B16)


def halve(t_ref, high_ref, low_ref):
    for k in range(t_ref.shape[0]):
        high_ref[k], low_ref[k] = split(t_ref[k])


def transposed_dot(x, y):
    return lax.dot_general(x, y, (((0,), (0,)), ((), ())), precision=HI, preferred_element_type=F32)


def contract(high_ref, low_ref, block_ref, sums_ref, piece_ref, gram_ref):
    x = lax.axis_index("x")
    ka = x * lax.axis_size("c") + lax.axis_index("c")
    depth, rows, cols = high_ref.shape
    rank = block_ref.shape[2] // 2
    wide = 2 * rank
    b = jnp.concatenate([block_ref[:, :-8, :rank], block_ref[:, :-8, rank:]], axis=1).reshape(-1, rank)
    c_wide = block_ref[:, -8:].reshape(-1, wide)
    gram_ref[...] = transposed_dot(b, jnp.concatenate([b, b], axis=1)) * transposed_dot(c_wide[:, :rank], c_wide)
    nothing = jnp.zeros(b.shape, B16)
    weights = []
    for k in range(depth):
        high, low = split(b * block_ref[ka, pl.ds(block_ref.shape[1] - 8 + k, 1), :rank])
        weights.append(
            (
                jnp.concatenate([high, low], axis=1),
                jnp.concatenate([high, nothing], axis=1),
                jnp.concatenate([low, high], axis=1),
                jnp.concatenate([nothing, high], axis=1),
            )
        )
    step = rows // 4
    lane = lax.broadcasted_iota(jnp.int32, (step, wide), 1)
    for at in range(0, rows // 2, step):
        sides = []
        for side in range(2):
            start = at + side * (rows // 2)
            first = jnp.zeros((step, wide), F32)
            second = jnp.zeros((step, wide), F32)
            for k in range(depth):
                first += jnp.dot(high_ref[k, start : start + step, :], weights[k][2 * side], preferred_element_type=F32)
                second += jnp.dot(low_ref[k, start : start + step, :], weights[k][2 * side + 1], preferred_element_type=F32)
            sides.append(first + (pltpu.roll(first, rank, 1) + second))
        sums_ref[at : at + step, :] = jnp.where(lane < rank, sides[0], sides[1])
    half = rank // 2
    lane = lax.broadcasted_iota(jnp.int32, (8, wide), 1)
    top = gram_ref[pl.ds(pl.multiple_of(8 * x, 8), 8), :]
    low = gram_ref[pl.ds(pl.multiple_of(half + 8 * x, 8), 8), :]
    moved = pltpu.roll(pltpu.roll(low, wide - half, 1), 4, 0)
    piece_ref[...] = jnp.where(lane < rank, jnp.where(lane < half, moved, low), top)


def compose(both_ref, piece_ref, out_ref):
    c = lax.axis_index("c")
    peers = out_ref.shape[0]
    wide = out_ref.shape[2]
    lane = lax.broadcasted_iota(jnp.int32, (8, wide), 1)
    sub = lax.broadcasted_iota(jnp.int32, (8, wide), 0)
    own = (sub < 4) & (lane < wide // 2)
    piece = piece_ref[...]
    for p in range(peers // 2):
        rows = both_ref[0, 8 * p : 8 * p + 8, :] + both_ref[1, 8 * p : 8 * p + 8, :]
        rows = jnp.where(c == 0, rows, pltpu.roll(rows, 4, 0))
        out_ref[p] = jnp.where(own, rows, piece)
        out_ref[p + peers // 2] = jnp.where(own, pltpu.roll(rows, wide // 2, 1), piece)


def inverse(x):
    r = pl.reciprocal(x, approx=True)
    r = r * (2.0 - x * r)
    return r * (2.0 - x * r)


def total(parts):
    while len(parts) > 1:
        parts = [x + y for x, y in zip(parts[::2], parts[1::2])]
    return parts[0]


def solve(n_x, got_ref, out_ref):
    wide = got_ref.shape[2]
    rank = wide // 2
    half = rank // 2
    n_ja = got_ref.shape[0] // n_x
    x = [total([got_ref[a * n_x + s] for a in range(n_ja)]) for s in range(n_x)]
    lane = lax.broadcasted_iota(jnp.int32, (8, wide), 1)
    sub = lax.broadcasted_iota(jnp.int32, (8, wide), 0)
    flipped = jnp.transpose(jnp.concatenate(x, axis=0))[rank + half :, :]
    groups = []
    for g in range(8):
        if g < 4:
            right = x[g]
        else:
            near = x[g - 4]
            corner = jnp.where(sub < 4, pltpu.roll(pltpu.roll(near, 4, 0), rank + half, 1), pltpu.roll(near, rank, 1))
            left = jnp.concatenate([flipped[8 * (g - 4) : 8 * (g - 3), :]] * 4, axis=1)
            right = jnp.where(lane < rank + half, left, corner)
        groups.append(jnp.where(lane < rank, jnp.where(lane == 8 * g + sub, 1.0, 0.0), right))
    m = pltpu.roll(total(x), rank, 1)
    groups.append(jnp.where((lane >= rank) & (sub < 4), m, 0.0))

    def column(a, c):
        return jnp.broadcast_to(a[:, c : c + 1], (8, wide))

    def row(a, r):
        return jnp.broadcast_to(a[r : r + 1, :], (8, wide))

    for r in range(8):
        at = rank + 8 * r
        own = groups[r]
        cols = [column(own, at + s) for s in range(8)]
        pivots = {(u, v): row(cols[v], u) for u in range(8) for v in range(u + 1)}
        rows = [row(own, s) for s in range(8)]
        left = {g: [column(groups[g], at + s) for s in range(8)] for g in range(r + 1, 9)}
        for t in range(8):
            inv = inverse(pivots[t, t])
            scaled = rows[t] * inv
            ratio = {u: pivots[u, t] * inv for u in range(t + 1, 8)}
            for u in range(t + 1, 8):
                for v in range(t + 1, u + 1):
                    pivots[u, v] = pivots[u, v] - ratio[u] * pivots[v, t]
            for u in range(t + 1, 8):
                rows[u] = rows[u] - ratio[u] * rows[t]
            for g in range(r + 1, 9):
                groups[g] = groups[g] - left[g][t] * scaled
                for u in range(t + 1, 8):
                    left[g][u] = left[g][u] - ratio[u] * left[g][t]
    out_ref[...] = -groups[8][: out_ref.shape[0], :rank]


def array(*shape, dtype=F32):
    return jax.ShapeDtypeStruct(shape, dtype)


def per_device(tensor, factor_b, factor_c):
    n_ja, n_x, n_c = lax.axis_size("ja"), lax.axis_size("x"), lax.axis_size("c")
    n_ka = n_x * n_c
    rows_b, rank = factor_b.shape
    rows = tensor.shape[1]
    mine = pl.pallas_call(
        functools.partial(spread, n_ka), out_shape=array(n_ka, rows_b // 2 + 8, 2 * rank), name="spread"
    )(factor_b, factor_c)
    high, low = pl.pallas_call(
        halve,
        out_shape=[array(*tensor.shape, dtype=B16)] * 2,
        compiler_params=BIG,
        cost_estimate=pl.CostEstimate(flops=2**21, bytes_accessed=2**22, transcendentals=0),
        name="halve",
    )(tensor)
    block = lax.all_to_all(mine, ("x", "c"), 0, 0, tiled=True)
    sums, piece = pl.pallas_call(
        contract,
        out_shape=[array(rows // 2, 2 * rank), array(8, 2 * rank)],
        scratch_shapes=[pltpu.VMEM((rank, 2 * rank), F32)],
        compiler_params=BIG,
        name="contract",
    )(high, low, block)
    both = lax.all_gather(sums, "c")
    packed = pl.pallas_call(
        compose, out_shape=array(n_ja * n_x, 8, 2 * rank), compiler_params=BIG, name="compose"
    )(both, piece)
    got = lax.all_to_all(packed, ("ja", "x"), 0, 0, tiled=True)
    return pl.pallas_call(
        functools.partial(solve, n_x), out_shape=array(rows // (n_ja * n_ka), rank), compiler_params=BIG, name="solve"
    )(got)


def solution(mesh):
    n = mesh.shape
    mesh = Mesh(mesh.devices.reshape(n["ia"], n["ja"], n["ka"] // 2, 2), ("ia", "ja", "x", "c"))
    ka = ("x", "c")
    in_specs = (P(ka, "ia", "ja"), P(("ja", *ka), None), P(ka, None))
    out_specs = P(("ia", "ja", *ka), None)
    return jax.shard_map(
        per_device, mesh=mesh, in_specs=in_specs, out_specs=out_specs, check_vma=False
    )
```

```python
import functools

import jax
import jax.numpy as jnp
from jax import lax
from jax.experimental import pallas as pl
from jax.experimental.pallas import tpu as pltpu
from jax.sharding import Mesh
from jax.sharding import PartitionSpec as P

HI = lax.Precision.HIGHEST
F32, B16 = jnp.float32, jnp.bfloat16
BIG = pltpu.CompilerParams(vmem_limit_bytes=32 * 2**20)


def spread(n_ka, b_ref, c_ref, out_ref, b_own, c_own, sems):
    copies = [pltpu.make_async_copy(b_ref, b_own, sems.at[0]), pltpu.make_async_copy(c_ref, c_own, sems.at[1])]
    for copy in copies:
        copy.start()
    for copy in copies:
        copy.wait()
    rows, rank = b_own.shape
    b = jnp.concatenate([b_own[: rows // 2], b_own[rows // 2 :]], axis=1)
    c = jnp.concatenate([c_own[...], jnp.zeros((8 - c_own.shape[0], rank), F32)], axis=0)
    c = jnp.concatenate([c, c], axis=1)
    for peer in range(n_ka):
        out_ref[peer, : rows // 2] = b
        out_ref[peer, rows // 2 :] = c


def split(x):
    high = x.astype(B16)
    return high, (x - high.astype(F32)).astype(B16)


def halve(t_ref, high_ref, low_ref):
    for k in range(t_ref.shape[0]):
        high_ref[k], low_ref[k] = split(t_ref[k])


def transposed_dot(x, y):
    return lax.dot_general(x, y, (((0,), (0,)), ((), ())), precision=HI, preferred_element_type=F32)


def contract(high_ref, low_ref, block_ref, sums_ref, piece_ref, gram_ref):
    x = lax.axis_index("x")
    ka = x * lax.axis_size("c") + lax.axis_index("c")
    depth, rows, cols = high_ref.shape
    rank = block_ref.shape[2] // 2
    wide = 2 * rank
    b = jnp.concatenate([block_ref[:, :-8, :rank], block_ref[:, :-8, rank:]], axis=1).reshape(-1, rank)
    c_wide = block_ref[:, -8:].reshape(-1, wide)
    gram_ref[...] = transposed_dot(b, jnp.concatenate([b, b], axis=1)) * transposed_dot(c_wide[:, :rank], c_wide)
    nothing = jnp.zeros(b.shape, B16)
    weights = []
    for k in range(depth):
        high, low = split(b * block_ref[ka, pl.ds(block_ref.shape[1] - 8 + k, 1), :rank])
        weights.append(
            (
                jnp.concatenate([high, low], axis=1),
                jnp.concatenate([high, nothing], axis=1),
                jnp.concatenate([low, high], axis=1),
                jnp.concatenate([nothing, high], axis=1),
            )
        )
    step = rows // 4
    lane = lax.broadcasted_iota(jnp.int32, (step, wide), 1)
    for at in range(0, rows // 2, step):
        sides = []
        for side in range(2):
            start = at + side * (rows // 2)
            first = jnp.zeros((step, wide), F32)
            second = jnp.zeros((step, wide), F32)
            for k in range(depth):
                first += jnp.dot(high_ref[k, start : start + step, :], weights[k][2 * side], preferred_element_type=F32)
                second += jnp.dot(low_ref[k, start : start + step, :], weights[k][2 * side + 1], preferred_element_type=F32)
            sides.append(first + (pltpu.roll(first, rank, 1) + second))
        sums_ref[at : at + step, :] = jnp.where(lane < rank, sides[0], sides[1])
    half = rank // 2
    lane = lax.broadcasted_iota(jnp.int32, (8, wide), 1)
    top = gram_ref[pl.ds(pl.multiple_of(8 * x, 8), 8), :]
    low = gram_ref[pl.ds(pl.multiple_of(half + 8 * x, 8), 8), :]
    moved = pltpu.roll(pltpu.roll(low, wide - half, 1), 4, 0)
    piece_ref[...] = jnp.where(lane < rank, jnp.where(lane < half, moved, low), top)


def compose(both_ref, piece_ref, out_ref):
    c = lax.axis_index("c")
    peers = out_ref.shape[0]
    wide = out_ref.shape[2]
    lane = lax.broadcasted_iota(jnp.int32, (8, wide), 1)
    sub = lax.broadcasted_iota(jnp.int32, (8, wide), 0)
    own = (sub < 4) & (lane < wide // 2)
    piece = piece_ref[...]
    for p in range(peers // 2):
        rows = both_ref[0, 8 * p : 8 * p + 8, :] + both_ref[1, 8 * p : 8 * p + 8, :]
        rows = jnp.where(c == 0, rows, pltpu.roll(rows, 4, 0))
        out_ref[p] = jnp.where(own, rows, piece)
        out_ref[p + peers // 2] = jnp.where(own, pltpu.roll(rows, wide // 2, 1), piece)


def total(parts):
    while len(parts) > 1:
        parts = [x + y for x, y in zip(parts[::2], parts[1::2])]
    return parts[0]


def solve(n_x, got_ref, out_ref):
    wide = got_ref.shape[2]
    rank = wide // 2
    half = rank // 2
    n_ja = got_ref.shape[0] // n_x
    x = [total([got_ref[a * n_x + s] for a in range(n_ja)]) for s in range(n_x)]
    lane = lax.broadcasted_iota(jnp.int32, (8, wide), 1)
    sub = lax.broadcasted_iota(jnp.int32, (8, wide), 0)
    flipped = jnp.transpose(jnp.concatenate(x, axis=0))[rank + half :, :]
    groups = []
    for g in range(8):
        if g < 4:
            right = x[g]
        else:
            near = x[g - 4]
            corner = jnp.where(sub < 4, pltpu.roll(pltpu.roll(near, 4, 0), rank + half, 1), pltpu.roll(near, rank, 1))
            left = jnp.concatenate([flipped[8 * (g - 4) : 8 * (g - 3), :]] * 4, axis=1)
            right = jnp.where(lane < rank + half, left, corner)
        groups.append(jnp.where(lane < rank, jnp.where(lane == 8 * g + sub, 1.0, 0.0), right))
    m = pltpu.roll(total(x), rank, 1)
    groups.append(jnp.where((lane >= rank) & (sub < 4), m, 0.0))

    def column(a, c):
        return jnp.take_along_axis(a, jnp.full((8, wide), c, jnp.int32), axis=1)

    def row(a, r):
        return jnp.take_along_axis(a, jnp.full((8, wide), r, jnp.int32), axis=0)

    for r in range(8):
        at = rank + 8 * r
        later = range(r + 1, 9)
        rows = [row(groups[r], s) for s in range(8)]
        pivots = {(u, v): column(rows[u], at + v) for u in range(8) for v in range(u + 1)}
        left = {g: [column(groups[g], at + s) for s in range(8)] for g in later}
        terms = {g: [] for g in later}
        for t in range(8):
            inv = 1.0 / pivots[t, t]
            scaled = rows[t] * inv
            ratio = {u: pivots[u, t] * inv for u in range(t + 1, 8)}
            for u in range(t + 1, 8):
                for v in range(t + 1, u + 1):
                    pivots[u, v] = pivots[u, v] - ratio[u] * pivots[v, t]
                rows[u] = rows[u] - ratio[u] * rows[t]
            for g in later:
                terms[g].append(left[g][t] * scaled)
                for u in range(t + 1, 8):
                    left[g][u] = left[g][u] - ratio[u] * left[g][t]
        for g in later:
            head, tail = terms[g][:4], terms[g][4:]
            groups[g] = groups[g] - (total(head) + (total(tail[:2]) + tail[2]) + tail[3])
    out_ref[...] = -groups[8][: out_ref.shape[0], :rank]


def array(*shape, dtype=F32):
    return jax.ShapeDtypeStruct(shape, dtype)


def per_device(tensor, factor_b, factor_c):
    n_ja, n_x, n_c = lax.axis_size("ja"), lax.axis_size("x"), lax.axis_size("c")
    n_ka = n_x * n_c
    rows_b, rank = factor_b.shape
    rows = tensor.shape[1]
    mine = pl.pallas_call(
        functools.partial(spread, n_ka),
        out_shape=array(n_ka, rows_b // 2 + 8, 2 * rank),
        in_specs=[pl.BlockSpec(memory_space=pl.ANY)] * 2,
        scratch_shapes=[
            pltpu.VMEM(factor_b.shape, F32),
            pltpu.VMEM(factor_c.shape, F32),
            pltpu.SemaphoreType.DMA((2,)),
        ],
        name="spread",
    )(factor_b, factor_c)
    high, low = pl.pallas_call(
        halve,
        out_shape=[array(*tensor.shape, dtype=B16)] * 2,
        compiler_params=BIG,
        cost_estimate=pl.CostEstimate(flops=2**21, bytes_accessed=2**22, transcendentals=0),
        name="halve",
    )(tensor)
    block = lax.all_to_all(mine, ("x", "c"), 0, 0, tiled=True)
    sums, piece = pl.pallas_call(
        contract,
        out_shape=[array(rows // 2, 2 * rank), array(8, 2 * rank)],
        scratch_shapes=[pltpu.VMEM((rank, 2 * rank), F32)],
        compiler_params=BIG,
        name="contract",
    )(high, low, block)
    both = lax.all_gather(sums, "c")
    packed = pl.pallas_call(
        compose, out_shape=array(n_ja * n_x, 8, 2 * rank), compiler_params=BIG, name="compose"
    )(both, piece)
    got = lax.all_to_all(packed, ("ja", "x"), 0, 0, tiled=True)
    return pl.pallas_call(
        functools.partial(solve, n_x), out_shape=array(rows // (n_ja * n_ka), rank), compiler_params=BIG, name="solve"
    )(got)


def solution(mesh):
    n = mesh.shape
    mesh = Mesh(mesh.devices.reshape(n["ia"], n["ja"], n["ka"] // 2, 2), ("ia", "ja", "x", "c"))
    ka = ("x", "c")
    in_specs = (P(ka, "ia", "ja"), P(("ja", *ka), None), P(ka, None))
    out_specs = P(("ia", "ja", *ka), None)
    return jax.shard_map(
        per_device, mesh=mesh, in_specs=in_specs, out_specs=out_specs, check_vma=False
    )
```

```python
import functools

import jax
import jax.numpy as jnp
from jax import lax
from jax.experimental import pallas as pl
from jax.experimental.pallas import tpu as pltpu
from jax.sharding import Mesh
from jax.sharding import PartitionSpec as P

HI = lax.Precision.HIGHEST
F32, B16 = jnp.float32, jnp.bfloat16
BIG = pltpu.CompilerParams(vmem_limit_bytes=32 * 2**20)


def spread(n_ka, b_ref, c_ref, out_ref, b_own, c_own, sems):
    copies = [pltpu.make_async_copy(b_ref, b_own, sems.at[0]), pltpu.make_async_copy(c_ref, c_own, sems.at[1])]
    for copy in copies:
        copy.start()
    for copy in copies:
        copy.wait()
    rows, rank = b_own.shape
    b = jnp.concatenate([b_own[: rows // 2], b_own[rows // 2 :]], axis=1)
    c = jnp.concatenate([c_own[...], jnp.zeros((8 - c_own.shape[0], rank), F32)], axis=0)
    c = jnp.concatenate([c, c], axis=1)
    for peer in range(n_ka):
        out_ref[peer, : rows // 2] = b
        out_ref[peer, rows // 2 :] = c


def split(x):
    high = x.astype(B16)
    return high, (x - high.astype(F32)).astype(B16)


def halve(t_ref, high_ref, low_ref):
    for k in range(t_ref.shape[0]):
        high_ref[k], low_ref[k] = split(t_ref[k])


def transposed_dot(x, y):
    return lax.dot_general(x, y, (((0,), (0,)), ((), ())), precision=HI, preferred_element_type=F32)


def contract(high_ref, low_ref, block_ref, sums_ref, piece_ref, gram_ref):
    x = lax.axis_index("x")
    ka = x * lax.axis_size("c") + lax.axis_index("c")
    depth, rows, cols = high_ref.shape
    rank = block_ref.shape[2] // 2
    wide = 2 * rank
    b = jnp.concatenate([block_ref[:, :-8, :rank], block_ref[:, :-8, rank:]], axis=1).reshape(-1, rank)
    c_wide = block_ref[:, -8:].reshape(-1, wide)
    gram_ref[...] = transposed_dot(b, jnp.concatenate([b, b], axis=1)) * transposed_dot(c_wide[:, :rank], c_wide)
    nothing = jnp.zeros(b.shape, B16)
    weights = []
    for k in range(depth):
        high, low = split(b * block_ref[ka, pl.ds(block_ref.shape[1] - 8 + k, 1), :rank])
        weights.append(
            (
                jnp.concatenate([high, low], axis=1),
                jnp.concatenate([high, nothing], axis=1),
                jnp.concatenate([low, high], axis=1),
                jnp.concatenate([nothing, high], axis=1),
            )
        )
    step = rows // 4
    lane = lax.broadcasted_iota(jnp.int32, (step, wide), 1)
    for at in range(0, rows // 2, step):
        sides = []
        for side in range(2):
            start = at + side * (rows // 2)
            first = jnp.zeros((step, wide), F32)
            second = jnp.zeros((step, wide), F32)
            for k in range(depth):
                first += jnp.dot(high_ref[k, start : start + step, :], weights[k][2 * side], preferred_element_type=F32)
                second += jnp.dot(low_ref[k, start : start + step, :], weights[k][2 * side + 1], preferred_element_type=F32)
            sides.append(first + (pltpu.roll(first, rank, 1) + second))
        sums_ref[at : at + step, :] = jnp.where(lane < rank, sides[0], sides[1])
    own = gram_ref[pl.ds(x, 16, stride=4), :]
    by16, by80, by96 = (pltpu.roll(own, n, 1) for n in (16, 80, 96))
    lane = lax.broadcasted_iota(jnp.int32, (1, wide), 1)

    def one(a, m):
        return a[m : m + 1, :]

    for r in range(4):
        piece_ref[r : r + 1, :] = one(own, r)
    for r in range(4, 7):
        left = jnp.where(lane < 16, one(by80, 15), one(own, 7))
        if r > 4:
            left = jnp.where(lane < 32, one(by96, 2 * r - 1), one(own, 2 * r - 2))
        right = jnp.where(lane < rank + 16, one(by16, r + 8), one(own, r))
        piece_ref[r : r + 1, :] = jnp.where(lane < rank, left, right)
    piece_ref[7:8, :] = jnp.zeros((1, wide), F32)


def compose(both_ref, piece_ref, out_ref):
    c = lax.axis_index("c")
    wide = out_ref.shape[1]
    half = both_ref.shape[1] // 8
    lane = lax.broadcasted_iota(jnp.int32, (half, wide), 1)
    for r in range(4):
        rows = both_ref[0, pl.ds(4 * c + r, half, stride=8), :] + both_ref[1, pl.ds(4 * c + r, half, stride=8), :]
        line = piece_ref[r : r + 1, :]
        out_ref[pl.ds(r, half, stride=7), :] = jnp.where(lane < wide // 2, rows, line)
        out_ref[pl.ds(7 * half + r, half, stride=7), :] = jnp.where(lane < wide // 2, pltpu.roll(rows, wide // 2, 1), line)
    for r in range(4, 7):
        out_ref[pl.ds(r, 2 * half, stride=7), :] = jnp.broadcast_to(piece_ref[r : r + 1, :], (2 * half, wide))


def total(parts):
    while len(parts) > 1:
        parts = [x + y for x, y in zip(parts[::2], parts[1::2])]
    return parts[0]


def solve(n_x, got_ref, out_ref, sum_ref):
    wide = got_ref.shape[1]
    rank = wide // 2
    two = 2 * 7 * n_x
    sum_ref[...] = total([got_ref[at : at + two, :] for at in range(0, got_ref.shape[0], two)])
    lane = lax.broadcasted_iota(jnp.int32, (8, wide), 1)
    sub = lax.broadcasted_iota(jnp.int32, (8, wide), 0)
    parts = [sum_ref[pl.ds(r, 8, stride=7), :] for r in range(7)]
    z = [part + pltpu.roll(part, 4, 0) for part in parts]
    by48 = [pltpu.roll(z[r], 48, 1) for r in (4, 5, 6)]
    by64 = [pltpu.roll(z[r], 64, 1) for r in (4, 5, 6)]
    by96 = [pltpu.roll(z[r], 96, 1) for r in (5, 6)]
    pieces = z[:7] + [by64[0], by64[1], by96[0], by64[2], by96[1]] + by48 + [pltpu.roll(z[4], 112, 1)]
    upper = [jnp.where(sub < 4, pieces[2 * g], pieces[2 * g + 1]) for g in range(8)]
    flipped = jnp.transpose(jnp.concatenate(upper, axis=0))[rank:, :]
    groups = []
    for g in range(8):
        left = flipped[8 * g : 8 * g + 8, :]
        right = jnp.where(lane < rank + 16 * (g // 2), jnp.concatenate([left, left], axis=1), upper[g]) if g > 1 else upper[g]
        groups.append(jnp.where(lane < rank, jnp.where(lane == 8 * g + sub, 1.0, 0.0), right))
    m = jnp.concatenate([jnp.sum(parts[r], axis=0, keepdims=True) for r in range(4)] + [jnp.zeros((4, wide), F32)], axis=0)
    groups.append(jnp.where(lane >= rank, pltpu.roll(m, rank, 1), 0.0))

    def column(a, c):
        return jnp.take_along_axis(a, jnp.full((8, wide), c, jnp.int32), axis=1)

    def row(a, r):
        return jnp.take_along_axis(a, jnp.full((8, wide), r, jnp.int32), axis=0)

    for r in range(8):
        at = rank + 8 * r
        later = range(r + 1, 9)
        rows = [row(groups[r], s) for s in range(8)]
        pivots = {(u, v): column(rows[u], at + v) for u in range(8) for v in range(u + 1)}
        left = {g: [column(groups[g], at + s) for s in range(8)] for g in later}
        terms = {g: [] for g in later}
        for t in range(8):
            inv = 1.0 / pivots[t, t]
            scaled = rows[t] * inv
            ratio = {u: pivots[u, t] * inv for u in range(t + 1, 8)}
            for u in range(t + 1, 8):
                for v in range(t + 1, u + 1):
                    pivots[u, v] = pivots[u, v] - ratio[u] * pivots[v, t]
                rows[u] = rows[u] - ratio[u] * rows[t]
            for g in later:
                terms[g].append(left[g][t] * scaled)
                for u in range(t + 1, 8):
                    left[g][u] = left[g][u] - ratio[u] * left[g][t]
        for g in later:
            head, tail = terms[g][:4], terms[g][4:]
            groups[g] = groups[g] - (total(head) + (total(tail[:2]) + tail[2]) + tail[3])
    out_ref[...] = -groups[8][: out_ref.shape[0], :rank]


def array(*shape, dtype=F32):
    return jax.ShapeDtypeStruct(shape, dtype)


def per_device(tensor, factor_b, factor_c):
    n_ja, n_x, n_c = lax.axis_size("ja"), lax.axis_size("x"), lax.axis_size("c")
    n_ka = n_x * n_c
    rows_b, rank = factor_b.shape
    rows = tensor.shape[1]
    mine = pl.pallas_call(
        functools.partial(spread, n_ka),
        out_shape=array(n_ka, rows_b // 2 + 8, 2 * rank),
        in_specs=[pl.BlockSpec(memory_space=pl.ANY)] * 2,
        scratch_shapes=[
            pltpu.VMEM(factor_b.shape, F32),
            pltpu.VMEM(factor_c.shape, F32),
            pltpu.SemaphoreType.DMA((2,)),
        ],
        name="spread",
    )(factor_b, factor_c)
    high, low = pl.pallas_call(
        halve,
        out_shape=[array(*tensor.shape, dtype=B16)] * 2,
        compiler_params=BIG,
        cost_estimate=pl.CostEstimate(flops=2**21, bytes_accessed=2**22, transcendentals=0),
        name="halve",
    )(tensor)
    block = lax.all_to_all(mine, ("x", "c"), 0, 0, tiled=True)
    sums, piece = pl.pallas_call(
        contract,
        out_shape=[array(rows // 2, 2 * rank), array(8, 2 * rank)],
        scratch_shapes=[pltpu.VMEM((rank, 2 * rank), F32)],
        compiler_params=BIG,
        name="contract",
    )(high, low, block)
    both = lax.all_gather(sums, "c")
    packed = pl.pallas_call(
        compose, out_shape=array(n_ja * n_x * 7, 2 * rank), compiler_params=BIG, name="compose"
    )(both, piece)
    got = lax.all_to_all(packed.reshape(n_ja * n_x, 1, 14 * rank), ("ja", "x"), 0, 0, tiled=True)
    return pl.pallas_call(
        functools.partial(solve, n_x),
        out_shape=array(rows // (n_ja * n_ka), rank),
        scratch_shapes=[pltpu.VMEM((14 * n_x, 2 * rank), F32)],
        compiler_params=BIG,
        name="solve",
    )(got.reshape(n_ja * n_x * 7, 2 * rank))


def solution(mesh):
    n = mesh.shape
    mesh = Mesh(mesh.devices.reshape(n["ia"], n["ja"], n["ka"] // 2, 2), ("ia", "ja", "x", "c"))
    ka = ("x", "c")
    in_specs = (P(ka, "ia", "ja"), P(("ja", *ka), None), P(ka, None))
    out_specs = P(("ia", "ja", *ka), None)
    return jax.shard_map(
        per_device, mesh=mesh, in_specs=in_specs, out_specs=out_specs, check_vma=False
    )
```

```python
import functools

import jax
import jax.numpy as jnp
from jax import lax
from jax.experimental import pallas as pl
from jax.experimental.pallas import tpu as pltpu
from jax.sharding import Mesh
from jax.sharding import PartitionSpec as P

HI = lax.Precision.HIGHEST
F32, B16 = jnp.float32, jnp.bfloat16
BIG = pltpu.CompilerParams(vmem_limit_bytes=32 * 2**20)


def spread(n_ka, b_ref, c_ref, out_ref, b_own, c_own, sems):
    copies = [pltpu.make_async_copy(b_ref, b_own, sems.at[0]), pltpu.make_async_copy(c_ref, c_own, sems.at[1])]
    for copy in copies:
        copy.start()
    for copy in copies:
        copy.wait()
    rows = b_own.shape[0]
    depth = c_own.shape[0]
    b = jnp.concatenate([b_own[: rows // 2], b_own[rows // 2 :]], axis=1)
    c = jnp.concatenate([c_own[: depth // 2], c_own[depth // 2 :]], axis=1)
    lines = (rows + depth) // 2
    for peer in range(n_ka):
        out_ref[lines * peer : lines * peer + rows // 2] = b
        out_ref[lines * peer + rows // 2 : lines * (peer + 1)] = c


def split(x):
    high = x.astype(B16)
    return high, (x - high.astype(F32)).astype(B16)


def halve(t_ref, high_ref, low_ref):
    for k in range(t_ref.shape[0]):
        high_ref[k], low_ref[k] = split(t_ref[k])


def transposed_dot(x, y):
    return lax.dot_general(x, y, (((0,), (0,)), ((), ())), precision=HI, preferred_element_type=F32)


def contract(high_ref, low_ref, block_ref, sums_ref, piece_ref, gram_ref):
    x = lax.axis_index("x")
    ka = x * lax.axis_size("c") + lax.axis_index("c")
    depth, rows, cols = high_ref.shape
    wide = block_ref.shape[1]
    rank = wide // 2
    n_ka = lax.axis_size("x") * lax.axis_size("c")
    lines = block_ref.shape[0] // n_ka
    b_lines = lines - depth // 2
    b = [block_ref[lines * peer : lines * peer + b_lines, :] for peer in range(n_ka)]
    b = jnp.concatenate([part[:, at : at + rank] for part in b for at in (0, rank)], axis=0)
    c_lines = [block_ref[pl.ds(b_lines + k, n_ka, stride=lines), :] for k in range(depth // 2)]
    c_lines = jnp.concatenate(c_lines + [pltpu.roll(line, rank, 1) for line in c_lines], axis=0)
    c_wide = jnp.concatenate([c_lines[:, :rank]] * 2, axis=1)
    b_wide = jnp.concatenate([b, b], axis=1)
    gram_ref[...] = transposed_dot(b, b_wide) * transposed_dot(c_wide[:, :rank], c_wide)
    column = lax.broadcasted_iota(jnp.int32, b_wide.shape, 1)
    weights = []
    for k in range(depth):
        c_own = block_ref[pl.ds(lines * ka + b_lines + k % (depth // 2), 1), :]
        turned = pltpu.roll(c_own, rank, 1)
        c_own = jnp.where((column[:1] < rank) == (k < depth // 2), c_own, turned)
        scaled = b_wide * c_own
        high = scaled.astype(B16)
        rounded = high.astype(F32)
        weights.append((jnp.where(column < rank, rounded, scaled - rounded).astype(B16), high))
    first = jnp.zeros((rows, wide), F32)
    for k in range(depth):
        first += jnp.dot(high_ref[k], weights[k][0], preferred_element_type=F32)
    second = jnp.zeros((rows, wide), F32)
    for k in range(depth):
        second += jnp.dot(low_ref[k], weights[k][1], preferred_element_type=F32)
    sums = first + (pltpu.roll(first, rank, 1) + second)
    lane = lax.broadcasted_iota(jnp.int32, (rows // 2, wide), 1)
    sums_ref[...] = jnp.where(lane < rank, sums[: rows // 2], sums[rows // 2 :])
    own = gram_ref[pl.ds(x, 16, stride=4), :]
    by16, by80, by96 = (pltpu.roll(own, n, 1) for n in (16, 80, 96))
    lane = lax.broadcasted_iota(jnp.int32, (1, wide), 1)

    def one(a, m):
        return a[m : m + 1, :]

    for r in range(4):
        piece_ref[r : r + 1, :] = one(own, r)
    for r in range(4, 7):
        left = jnp.where(lane < 16, one(by80, 15), one(own, 7))
        if r > 4:
            left = jnp.where(lane < 32, one(by96, 2 * r - 1), one(own, 2 * r - 2))
        right = jnp.where(lane < rank + 16, one(by16, r + 8), one(own, r))
        piece_ref[r : r + 1, :] = jnp.where(lane < rank, left, right)
    piece_ref[7:8, :] = jnp.zeros((1, wide), F32)


def compose(both_ref, piece_ref, out_ref):
    c = lax.axis_index("c")
    wide = out_ref.shape[1]
    half = both_ref.shape[1] // 8
    lane = lax.broadcasted_iota(jnp.int32, (half, wide), 1)
    for r in range(4):
        rows = both_ref[0, pl.ds(4 * c + r, half, stride=8), :] + both_ref[1, pl.ds(4 * c + r, half, stride=8), :]
        line = piece_ref[r : r + 1, :]
        out_ref[pl.ds(r, half, stride=7), :] = jnp.where(lane < wide // 2, rows, line)
        out_ref[pl.ds(7 * half + r, half, stride=7), :] = jnp.where(lane < wide // 2, pltpu.roll(rows, wide // 2, 1), line)
    for r in range(4, 7):
        out_ref[pl.ds(r, 2 * half, stride=7), :] = jnp.broadcast_to(piece_ref[r : r + 1, :], (2 * half, wide))


def total(parts):
    while len(parts) > 1:
        parts = [x + y for x, y in zip(parts[::2], parts[1::2])]
    return parts[0]


def solve(n_x, got_ref, out_ref, sum_ref):
    wide = got_ref.shape[1]
    rank = wide // 2
    two = 2 * 7 * n_x
    sum_ref[...] = total([got_ref[at : at + two, :] for at in range(0, got_ref.shape[0], two)])
    lane = lax.broadcasted_iota(jnp.int32, (8, wide), 1)
    sub = lax.broadcasted_iota(jnp.int32, (8, wide), 0)
    parts = [sum_ref[pl.ds(r, 8, stride=7), :] for r in range(7)]
    z = [part + pltpu.roll(part, 4, 0) for part in parts]
    by48 = [pltpu.roll(z[r], 48, 1) for r in (4, 5, 6)]
    by64 = [pltpu.roll(z[r], 64, 1) for r in (4, 5, 6)]
    by96 = [pltpu.roll(z[r], 96, 1) for r in (5, 6)]
    pieces = z[:7] + [by64[0], by64[1], by96[0], by64[2], by96[1]] + by48 + [pltpu.roll(z[4], 112, 1)]
    upper = [jnp.where(sub < 4, pieces[2 * g], pieces[2 * g + 1]) for g in range(8)]
    flipped = jnp.transpose(jnp.concatenate(upper, axis=0))[rank:, :]
    groups = []
    for g in range(8):
        left = flipped[8 * g : 8 * g + 8, :]
        right = jnp.where(lane < rank + 16 * (g // 2), jnp.concatenate([left, left], axis=1), upper[g]) if g > 1 else upper[g]
        groups.append(jnp.where(lane < rank, jnp.where(lane == 8 * g + sub, 1.0, 0.0), right))
    m = jnp.concatenate([jnp.sum(parts[r], axis=0, keepdims=True) for r in range(4)] + [jnp.zeros((4, wide), F32)], axis=0)
    groups.append(jnp.where(lane >= rank, pltpu.roll(m, rank, 1), 0.0))

    def column(a, c):
        return jnp.take_along_axis(a, jnp.full((8, wide), c, jnp.int32), axis=1)

    def row(a, r):
        return jnp.take_along_axis(a, jnp.full((8, wide), r, jnp.int32), axis=0)

    rows = [row(groups[0], s) for s in range(8)]
    for r in range(8):
        at = rank + 8 * r
        later = range(r + 1, 9)
        pivots = {(u, v): column(rows[u], at + v) for u in range(8) for v in range(u + 1)}
        left = {g: [column(groups[g], at + s) for s in range(8)] for g in later}
        terms = {g: [] for g in later}
        following = None
        for t in range(8):
            if t == 6 and r < 7:
                for term in terms[r + 1]:
                    groups[r + 1] = groups[r + 1] - term
                following = [row(groups[r + 1], s) for s in range(8)]
            inv = 1.0 / pivots[t, t]
            scaled = rows[t] * inv
            ratio = {u: pivots[u, t] * inv for u in range(t + 1, 8)}
            for u in range(t + 1, 8):
                for v in range(t + 1, u + 1):
                    pivots[u, v] = pivots[u, v] - ratio[u] * pivots[v, t]
                rows[u] = rows[u] - ratio[u] * rows[t]
            for g in later:
                if following is not None and g == r + 1:
                    following = [following[s] - row(left[g][t], s) * scaled for s in range(8)]
                else:
                    terms[g].append(left[g][t] * scaled)
                for u in range(t + 1, 8):
                    left[g][u] = left[g][u] - ratio[u] * left[g][t]
        for g in later:
            if following is None or g > r + 1:
                head, tail = terms[g][:4], terms[g][4:]
                groups[g] = groups[g] - (total(head) + (total(tail[:2]) + tail[2]) + tail[3])
        rows = following
    out_ref[...] = -groups[8][: out_ref.shape[0], :rank]


def array(*shape, dtype=F32):
    return jax.ShapeDtypeStruct(shape, dtype)


def per_device(tensor, factor_b, factor_c):
    n_ja, n_x, n_c = lax.axis_size("ja"), lax.axis_size("x"), lax.axis_size("c")
    n_ka = n_x * n_c
    rows_b, rank = factor_b.shape
    rows = tensor.shape[1]
    lines = (rows_b + factor_c.shape[0]) // 2
    mine = pl.pallas_call(
        functools.partial(spread, n_ka),
        out_shape=array(n_ka * lines, 2 * rank),
        in_specs=[pl.BlockSpec(memory_space=pl.ANY)] * 2,
        scratch_shapes=[
            pltpu.VMEM(factor_b.shape, F32),
            pltpu.VMEM(factor_c.shape, F32),
            pltpu.SemaphoreType.DMA((2,)),
        ],
        name="spread",
    )(factor_b, factor_c)
    high, low = pl.pallas_call(
        halve,
        out_shape=[array(*tensor.shape, dtype=B16)] * 2,
        compiler_params=BIG,
        cost_estimate=pl.CostEstimate(flops=2**21, bytes_accessed=2**22, transcendentals=0),
        name="halve",
    )(tensor)
    block = lax.all_to_all(mine.reshape(n_ka, 1, lines * 2 * rank), ("x", "c"), 0, 0, tiled=True)
    sums, piece = pl.pallas_call(
        contract,
        out_shape=[array(rows // 2, 2 * rank), array(8, 2 * rank)],
        scratch_shapes=[pltpu.VMEM((rank, 2 * rank), F32)],
        compiler_params=BIG,
        name="contract",
    )(high, low, block.reshape(n_ka * lines, 2 * rank))
    both = lax.all_gather(sums, "c")
    packed = pl.pallas_call(
        compose, out_shape=array(n_ja * n_x * 7, 2 * rank), compiler_params=BIG, name="compose"
    )(both, piece)
    got = lax.all_to_all(packed.reshape(n_ja * n_x, 1, 14 * rank), ("ja", "x"), 0, 0, tiled=True)
    return pl.pallas_call(
        functools.partial(solve, n_x),
        out_shape=array(rows // (n_ja * n_ka), rank),
        scratch_shapes=[pltpu.VMEM((14 * n_x, 2 * rank), F32)],
        compiler_params=BIG,
        name="solve",
    )(got.reshape(n_ja * n_x * 7, 2 * rank))


def solution(mesh):
    n = mesh.shape
    mesh = Mesh(mesh.devices.reshape(n["ia"], n["ja"], n["ka"] // 2, 2), ("ia", "ja", "x", "c"))
    ka = ("x", "c")
    in_specs = (P(ka, "ia", "ja"), P(("ja", *ka), None), P(ka, None))
    out_specs = P(("ia", "ja", *ka), None)
    return jax.shard_map(
        per_device, mesh=mesh, in_specs=in_specs, out_specs=out_specs, check_vma=False
    )
```

```python
import functools

import jax
import jax.numpy as jnp
from jax import lax
from jax.experimental import pallas as pl
from jax.experimental.pallas import tpu as pltpu
from jax.sharding import Mesh
from jax.sharding import PartitionSpec as P

HI = lax.Precision.HIGHEST
F32, B16 = jnp.float32, jnp.bfloat16
BIG = pltpu.CompilerParams(vmem_limit_bytes=32 * 2**20)


def spread(n_ka, b_ref, c_ref, out_ref, b_own, c_own, sems):
    copies = [pltpu.make_async_copy(b_ref, b_own, sems.at[0]), pltpu.make_async_copy(c_ref, c_own, sems.at[1])]
    for copy in copies:
        copy.start()
    for copy in copies:
        copy.wait()
    rows, rank = b_own.shape
    b = jnp.concatenate([b_own[: rows // 2], b_own[rows // 2 :]], axis=1)
    c = jnp.concatenate([c_own[...], jnp.zeros((8 - c_own.shape[0], rank), F32)], axis=0)
    c = jnp.concatenate([c, c], axis=1)
    for peer in range(n_ka):
        out_ref[peer, : rows // 2] = b
        out_ref[peer, rows // 2 :] = c


def split(x):
    high = x.astype(B16)
    return high, (x - high.astype(F32)).astype(B16)


def halve(t_ref, high_ref, low_ref):
    for k in range(t_ref.shape[0]):
        high_ref[k], low_ref[k] = split(t_ref[k])


def transposed_dot(x, y):
    return lax.dot_general(x, y, (((0,), (0,)), ((), ())), precision=HI, preferred_element_type=F32)


def contract(high_ref, low_ref, block_ref, sums_ref, piece_ref, gram_ref):
    x = lax.axis_index("x")
    ka = x * lax.axis_size("c") + lax.axis_index("c")
    depth, rows, cols = high_ref.shape
    rank = block_ref.shape[2] // 2
    wide = 2 * rank
    b = jnp.concatenate([block_ref[:, :-8, :rank], block_ref[:, :-8, rank:]], axis=1).reshape(-1, rank)
    c_wide = block_ref[:, -8:].reshape(-1, wide)
    b_wide = jnp.concatenate([b, b], axis=1)
    gram_ref[...] = transposed_dot(b, b_wide) * transposed_dot(c_wide[:, :rank], c_wide)
    column = lax.broadcasted_iota(jnp.int32, b_wide.shape, 1)
    weights = []
    for k in range(depth):
        scaled = b_wide * block_ref[ka, pl.ds(block_ref.shape[1] - 8 + k, 1), :]
        high = scaled.astype(B16)
        rounded = high.astype(F32)
        weights.append((jnp.where(column < rank, rounded, scaled - rounded).astype(B16), high))
    first = jnp.zeros((rows, wide), F32)
    for k in range(depth):
        first += jnp.dot(high_ref[k], weights[k][0], preferred_element_type=F32)
    second = jnp.zeros((rows, wide), F32)
    for k in range(depth):
        second += jnp.dot(low_ref[k], weights[k][1], preferred_element_type=F32)
    sums = first + (pltpu.roll(first, rank, 1) + second)
    lane = lax.broadcasted_iota(jnp.int32, (rows // 2, wide), 1)
    sums_ref[...] = jnp.where(lane < rank, sums[: rows // 2], sums[rows // 2 :])
    own = gram_ref[pl.ds(x, 16, stride=4), :]
    by16, by80, by96 = (pltpu.roll(own, n, 1) for n in (16, 80, 96))
    lane = lax.broadcasted_iota(jnp.int32, (1, wide), 1)

    def one(a, m):
        return a[m : m + 1, :]

    for r in range(4):
        piece_ref[r : r + 1, :] = one(own, r)
    for r in range(4, 7):
        left = jnp.where(lane < 16, one(by80, 15), one(own, 7))
        if r > 4:
            left = jnp.where(lane < 32, one(by96, 2 * r - 1), one(own, 2 * r - 2))
        right = jnp.where(lane < rank + 16, one(by16, r + 8), one(own, r))
        piece_ref[r : r + 1, :] = jnp.where(lane < rank, left, right)
    piece_ref[7:8, :] = jnp.zeros((1, wide), F32)


def compose(both_ref, piece_ref, out_ref):
    c = lax.axis_index("c")
    wide = out_ref.shape[1]
    half = both_ref.shape[1] // 8
    lane = lax.broadcasted_iota(jnp.int32, (half, wide), 1)
    for r in range(4):
        rows = both_ref[0, pl.ds(4 * c + r, half, stride=8), :] + both_ref[1, pl.ds(4 * c + r, half, stride=8), :]
        line = piece_ref[r : r + 1, :]
        out_ref[pl.ds(r, half, stride=7), :] = jnp.where(lane < wide // 2, rows, line)
        out_ref[pl.ds(7 * half + r, half, stride=7), :] = jnp.where(lane < wide // 2, pltpu.roll(rows, wide // 2, 1), line)
    for r in range(4, 7):
        out_ref[pl.ds(r, 2 * half, stride=7), :] = jnp.broadcast_to(piece_ref[r : r + 1, :], (2 * half, wide))


def total(parts):
    while len(parts) > 1:
        parts = [x + y for x, y in zip(parts[::2], parts[1::2])]
    return parts[0]


def solve(n_x, got_ref, out_ref, sum_ref):
    wide = got_ref.shape[1]
    rank = wide // 2
    two = 2 * 7 * n_x
    sum_ref[...] = total([got_ref[at : at + two, :] for at in range(0, got_ref.shape[0], two)])
    lane = lax.broadcasted_iota(jnp.int32, (8, wide), 1)
    sub = lax.broadcasted_iota(jnp.int32, (8, wide), 0)
    parts = [sum_ref[pl.ds(r, 8, stride=7), :] for r in range(7)]
    z = [part + pltpu.roll(part, 4, 0) for part in parts]
    by48 = [pltpu.roll(z[r], 48, 1) for r in (4, 5, 6)]
    by64 = [pltpu.roll(z[r], 64, 1) for r in (4, 5, 6)]
    by96 = [pltpu.roll(z[r], 96, 1) for r in (5, 6)]
    pieces = z[:7] + [by64[0], by64[1], by96[0], by64[2], by96[1]] + by48 + [pltpu.roll(z[4], 112, 1)]
    upper = [jnp.where(sub < 4, pieces[2 * g], pieces[2 * g + 1]) for g in range(8)]
    flipped = jnp.transpose(jnp.concatenate(upper, axis=0))[rank:, :]
    groups = []
    for g in range(8):
        left = flipped[8 * g : 8 * g + 8, :]
        right = jnp.where(lane < rank + 16 * (g // 2), jnp.concatenate([left, left], axis=1), upper[g]) if g > 1 else upper[g]
        groups.append(jnp.where(lane < rank, jnp.where(lane == 8 * g + sub, 1.0, 0.0), right))
    m = jnp.concatenate([jnp.sum(parts[r], axis=0, keepdims=True) for r in range(4)] + [jnp.zeros((4, wide), F32)], axis=0)
    groups.append(jnp.where(lane >= rank, pltpu.roll(m, rank, 1), 0.0))

    def column(a, c):
        return jnp.take_along_axis(a, jnp.full((8, wide), c, jnp.int32), axis=1)

    def row(a, r):
        return jnp.take_along_axis(a, jnp.full((8, wide), r, jnp.int32), axis=0)

    for r in range(8):
        at = rank + 8 * r
        later = range(r + 1, 9)
        rows = [row(groups[r], s) for s in range(8)]
        pivots = {(u, v): column(rows[u], at + v) for u in range(8) for v in range(u + 1)}
        left = {g: [column(groups[g], at + s) for s in range(8)] for g in later}
        terms = {g: [] for g in later}
        for t in range(8):
            inv = 1.0 / pivots[t, t]
            scaled = rows[t] * inv
            ratio = {u: pivots[u, t] * inv for u in range(t + 1, 8)}
            for u in range(t + 1, 8):
                for v in range(t + 1, u + 1):
                    pivots[u, v] = pivots[u, v] - ratio[u] * pivots[v, t]
                rows[u] = rows[u] - ratio[u] * rows[t]
            for g in later:
                terms[g].append(left[g][t] * scaled)
                for u in range(t + 1, 8):
                    left[g][u] = left[g][u] - ratio[u] * left[g][t]
        for g in later:
            head, tail = terms[g][:4], terms[g][4:]
            groups[g] = groups[g] - (total(head) + (total(tail[:2]) + tail[2]) + tail[3])
    out_ref[...] = -groups[8][: out_ref.shape[0], :rank]


def array(*shape, dtype=F32):
    return jax.ShapeDtypeStruct(shape, dtype)


def per_device(tensor, factor_b, factor_c):
    n_ja, n_x, n_c = lax.axis_size("ja"), lax.axis_size("x"), lax.axis_size("c")
    n_ka = n_x * n_c
    rows_b, rank = factor_b.shape
    rows = tensor.shape[1]
    mine = pl.pallas_call(
        functools.partial(spread, n_ka),
        out_shape=array(n_ka, rows_b // 2 + 8, 2 * rank),
        in_specs=[pl.BlockSpec(memory_space=pl.ANY)] * 2,
        scratch_shapes=[
            pltpu.VMEM(factor_b.shape, F32),
            pltpu.VMEM(factor_c.shape, F32),
            pltpu.SemaphoreType.DMA((2,)),
        ],
        name="spread",
    )(factor_b, factor_c)
    high, low = pl.pallas_call(
        halve,
        out_shape=[array(*tensor.shape, dtype=B16)] * 2,
        compiler_params=BIG,
        cost_estimate=pl.CostEstimate(flops=2**21, bytes_accessed=2**22, transcendentals=0),
        name="halve",
    )(tensor)
    block = lax.all_to_all(mine, ("x", "c"), 0, 0, tiled=True)
    sums, piece = pl.pallas_call(
        contract,
        out_shape=[array(rows // 2, 2 * rank), array(8, 2 * rank)],
        scratch_shapes=[pltpu.VMEM((rank, 2 * rank), F32)],
        compiler_params=BIG,
        name="contract",
    )(high, low, block)
    both = lax.all_gather(sums, "c")
    packed = pl.pallas_call(
        compose, out_shape=array(n_ja * n_x * 7, 2 * rank), compiler_params=BIG, name="compose"
    )(both, piece)
    got = lax.all_to_all(packed.reshape(n_ja * n_x, 1, 14 * rank), ("ja", "x"), 0, 0, tiled=True)
    return pl.pallas_call(
        functools.partial(solve, n_x),
        out_shape=array(rows // (n_ja * n_ka), rank),
        scratch_shapes=[pltpu.VMEM((14 * n_x, 2 * rank), F32)],
        compiler_params=BIG,
        name="solve",
    )(got.reshape(n_ja * n_x * 7, 2 * rank))


def solution(mesh):
    n = mesh.shape
    mesh = Mesh(mesh.devices.reshape(n["ia"], n["ja"], n["ka"] // 2, 2), ("ia", "ja", "x", "c"))
    ka = ("x", "c")
    in_specs = (P(ka, "ia", "ja"), P(("ja", *ka), None), P(ka, None))
    out_specs = P(("ia", "ja", *ka), None)
    return jax.shard_map(
        per_device, mesh=mesh, in_specs=in_specs, out_specs=out_specs, check_vma=False
    )
```
